128 devices in a mesh: leaf: 64 (over y, x, z), rhs: 2 (over core).
Axes of the slice: x: 4, y: 4, z: 4, core: 2. Of those that a mesh axis runs over, the one named last changes fastest.
Arguments:
- operand: bfloat16 [262144, 128], P('leaf', 'rhs'), may hold values from -6 to 6
- near_blocks: bfloat16 [8192, 256, 256], P(('leaf', 'rhs')), may hold values from -0.125 to 0.125
- near_row: int32 [8192], P(('leaf', 'rhs')), may hold values from 0 to 1023, as said below
- near_column: int32 [8192], P(('leaf', 'rhs')), may hold values from 0 to 1023, as said below
- row_basis: bfloat16 [1024, 256, 64], P('leaf'), may hold values from -0.375 to 0.375
- leaf_column_bases: bfloat16 [1024, 256, 64], P('leaf'), may hold values from -0.4375 to 0.4375
- lift_leaf: bfloat16 [1024, 64, 64], P('leaf'), may hold values from -0.5 to 0.5
- lift_middle: bfloat16 [512, 64, 64], P('leaf'), may hold values from -0.5 to 0.5
- spread_middle: bfloat16 [512, 64, 64], P('leaf'), may hold values from -0.75 to 0.75
- spread_leaf: bfloat16 [1024, 64, 64], P('leaf'), may hold values from -0.75 to 0.75
- couple_leaf: bfloat16 [1024, 16, 64, 64], P('leaf'), may hold values from -0.25 to 0.25
- couple_middle: bfloat16 [512, 16, 64, 64], P('leaf'), may hold values from -0.25 to 0.25
- couple_top: bfloat16 [256, 16, 64, 64], P('leaf'), may hold values from -0.25 to 0.25
- list_leaf: int32 [1024, 16], P('leaf'), may hold values from 0 to 1023, as said below
- list_middle: int32 [512, 16], P('leaf'), may hold values from 0 to 511, as said below
- list_top: int32 [256, 16], P('leaf'), may hold values from 0 to 255, as said below
- count_leaf: int32 [1024], P('leaf'), may hold values from 1 to 16, as said below
- count_middle: int32 [512], P('leaf'), may hold values from 1 to 16, as said below
- count_top: int32 [256], P('leaf'), may hold values from 1 to 16, as said below
Outputs:
- adjoint: bfloat16 [262144, 128], P('leaf', 'rhs')
The draws below stay inside these ranges and needn't reach their ends.
Inputs may be any that keep to these rules, and one draw needn't show every extreme that they name: near_row of the blocks held by index i of leaf (rows i * 8 * 16 to (i + 1) * 8 * 16 - 1) lies in i * 16 to (i + 1) * 16 - 1; counts per leaf row are uneven. near_column of a block held by index i of leaf lies in i * 16 - 8 to (i + 1) * 16 + 7. `list_leaf`: a leaf cluster t of index i = t // 16 lists only leaf clusters of the indices i - 1, i and i + 1. `list_middle`: a middle cluster t of index i = t // 8 lists only middle clusters of the indices i - 2 to i + 2. `list_top`: a top cluster t of index i = t // 4 lists only top clusters of the indices i - 4 to i + 4. `count_leaf`: slots from count on are not used. `count_middle`: slots from count on are not used. `count_top`: slots from count on are not used.
All inputs are finite; a program needn't handle non-finite values.
Results may differ from the reference program's by a relative error of at most 0.005.
Values may be sent and summed in bfloat16 or wider, within the bound.
No kernel may reach another device: no remote copies, remote signals or barrier semaphores. Data moves between devices by JAX's collectives and lax.ppermute only.
A program may use at most 128 MiB of HBM per device.

```python
import jax
import jax.numpy as jnp
from jax import lax

LEAF = 256
K = 64
RHS = 128
NEAR = 8
FAR = 16
L_DEV = 16
HW = 8
LEAVES = 1024
N_LEAF = 64
N_RHS = 2


def spread_ints(key, lowest, highest, shape):
    random_int = jax.random.randint(key, shape, 0, 1 << 20)
    return lowest + random_int % (highest - lowest)


def draw_near_row(key, part):
    key = jax.random.fold_in(key, 11)
    index_all = jnp.arange(NEAR * LEAVES)
    owner = index_all // (NEAR * L_DEV)
    values = owner * L_DEV + jax.random.randint(key, (NEAR * LEAVES,), 0, L_DEV)
    values = values.at[0].set(0).at[NEAR * LEAVES - 1].set(LEAVES - 1)
    return values.astype(jnp.int32)


def draw_near_column(key, part):
    key = jax.random.fold_in(key, 12)
    index_all = jnp.arange(NEAR * LEAVES)
    owner = index_all // (NEAR * L_DEV)
    lowest = jnp.maximum(0, owner * L_DEV - HW)
    highest = jnp.minimum(LEAVES, (owner + 1) * L_DEV + HW)
    values = spread_ints(key, lowest, highest, (NEAR * LEAVES,))
    values = values.at[0].set(0).at[NEAR * LEAVES - 1].set(LEAVES - 1)
    return values.astype(jnp.int32)


def local_list(key, clusters, per_device, reach):
    target = jnp.arange(clusters)
    owner = target // per_device
    lowest = jnp.maximum(0, (owner - reach) * per_device)[:, None]
    highest = jnp.minimum(clusters, (owner + reach + 1) * per_device)[:, None]
    values = spread_ints(key, lowest, highest, (clusters, FAR))
    values = values.at[0, 0].set(0).at[clusters - 1, 0].set(clusters - 1)
    return values.astype(jnp.int32)


def draw_list_leaf(key, part):
    key = jax.random.fold_in(key, 13)
    return local_list(key, LEAVES, L_DEV, 1)


def draw_list_middle(key, part):
    key = jax.random.fold_in(key, 14)
    return local_list(key, LEAVES // 2, L_DEV // 2, 2)


def draw_list_top(key, part):
    key = jax.random.fold_in(key, 15)
    return local_list(key, LEAVES // 4, L_DEV // 4, 4)


def live_counts(key, clusters):
    values = jax.random.randint(key, (clusters,), 1, FAR + 1)
    values = values.at[0].set(FAR).at[1].set(1)
    return values.astype(jnp.int32)


def draw_count_leaf(key, part):
    key = jax.random.fold_in(key, 16)
    return live_counts(key, LEAVES)


def draw_count_middle(key, part):
    key = jax.random.fold_in(key, 17)
    return live_counts(key, LEAVES // 2)


def draw_count_top(key, part):
    key = jax.random.fold_in(key, 18)
    return live_counts(key, LEAVES // 4)


def levels(rng, shape, cuts, smallest, largest):
    def one(axis_at, parts):
        steps = jax.random.uniform(jax.random.fold_in(jax.random.fold_in(rng, 6), axis_at), (parts,), jnp.float32, smallest / len(cuts), largest / len(cuts))
        return jnp.repeat(jnp.exp(steps), shape[axis_at] // parts).reshape((-1,) + (1,) * (len(shape) - axis_at - 1))

    loudness = one(*cuts[0])
    for cut in cuts[1:]:
        loudness = loudness * one(*cut)
    return loudness


def centred(stream_key, dims, scale, most, shards=(), kind=jnp.bfloat16):
    loudness = levels(stream_key, dims, shards, -0.22, 0.18) if shards else 1.0
    result = jax.random.normal(stream_key, dims, jnp.float32) * scale * loudness
    return jnp.minimum(jnp.maximum(result, -most), most).astype(kind)


def setup_inputs(seed: int = 0) -> dict:
    key_of = jax.random.split(jax.random.key(seed), 20)
    return {
        "operand": centred(key_of[0], (LEAVES * LEAF, RHS), 1.0, 6.0, ((0, 64), (1, 2))),
        "near_blocks": centred(key_of[1], (NEAR * LEAVES, LEAF, LEAF), (NEAR * LEAF) ** -0.5, 0.125, ((0, 128),)),
        "near_row": draw_near_row(jax.random.fold_in(key_of[19], 71), 0),
        "near_column": draw_near_column(jax.random.fold_in(key_of[19], 71), 0),
        "row_basis": centred(key_of[4], (LEAVES, LEAF, K), LEAF ** -0.5, 0.375, ((0, 64),)),
        "leaf_column_bases": centred(key_of[5], (LEAVES, LEAF, K), (3 * K) ** -0.5, 0.4375, ((0, 64),)),
        "lift_leaf": centred(key_of[6], (LEAVES, K, K), (2 * K) ** -0.5, 0.5, ((0, 64),)),
        "lift_middle": centred(key_of[7], (LEAVES // 2, K, K), (2 * K) ** -0.5, 0.5, ((0, 64),)),
        "spread_middle": centred(key_of[8], (LEAVES // 2, K, K), K ** -0.5, 0.75, ((0, 64),)),
        "spread_leaf": centred(key_of[9], (LEAVES, K, K), K ** -0.5, 0.75, ((0, 64),)),
        "couple_leaf": centred(key_of[10], (LEAVES, FAR, K, K), (K * FAR // 2) ** -0.5, 0.25, ((0, 64),)),
        "couple_middle": centred(key_of[11], (LEAVES // 2, FAR, K, K), (K * FAR // 2) ** -0.5, 0.25, ((0, 64),)),
        "couple_top": centred(key_of[12], (LEAVES // 4, FAR, K, K), (K * FAR // 2) ** -0.5, 0.25, ((0, 64),)),
        "list_leaf": draw_list_leaf(jax.random.fold_in(key_of[19], 71), 0),
        "list_middle": draw_list_middle(jax.random.fold_in(key_of[19], 71), 0),
        "list_top": draw_list_top(jax.random.fold_in(key_of[19], 71), 0),
        "count_leaf": draw_count_leaf(jax.random.fold_in(key_of[19], 71), 0),
        "count_middle": draw_count_middle(jax.random.fold_in(key_of[19], 71), 0),
        "count_top": draw_count_top(jax.random.fold_in(key_of[19], 71), 0),
    }


def couple_level(coeffs, blocks, sources, entry_counts):
    picked = jnp.take(coeffs, sources, axis=0)
    live_slot = jnp.arange(sources.shape[1])[None, :] < entry_counts[:, None]
    picked = jnp.where(live_slot[:, :, None, None], picked, jnp.zeros((), picked.dtype))
    return jnp.einsum("tjkm,tjkr->tmr", blocks.astype(jnp.float32), picked.astype(jnp.float32))


def descend(transfer, parent):
    pairs = transfer.shape[0] // 2
    shaped = transfer.reshape(pairs, 2, K, K).astype(jnp.float32)
    spread = jnp.einsum("pcmn,pnr->pcmr", shaped, parent, precision=lax.Precision.HIGHEST)
    return spread.reshape(2 * pairs, K, parent.shape[2])


def lift(transfer, child):
    pairs = transfer.shape[0] // 2
    shaped = transfer.reshape(pairs, 2, K, K).astype(jnp.float32)
    kids = child.reshape(pairs, 2, K, child.shape[2]).astype(jnp.float32)
    return jnp.einsum("pckm,pckr->pmr", shaped, kids).astype(jnp.bfloat16)


def reference(operand, near_blocks, near_row, near_column, row_basis, leaf_column_bases, lift_leaf, lift_middle, spread_middle, spread_leaf, couple_leaf, couple_middle, couple_top, list_leaf, list_middle, list_top, count_leaf, count_middle, count_top):
    blocked = operand.reshape(LEAVES, LEAF, RHS)
    groups = N_LEAF * N_RHS
    per_group = NEAR * LEAVES // groups

    def near_step(running, pieces):
        tiles, row_indices, col_ids = pieces
        picked = jnp.take(blocked, row_indices, axis=0).astype(jnp.float32)
        product = jnp.einsum("bij,bir->bjr", tiles.astype(jnp.float32), picked)
        return running.at[col_ids].add(product), None

    start = jnp.zeros((LEAVES, LEAF, RHS), jnp.float32)
    nearfield_sum, unused = lax.scan(near_step, start, (near_blocks.reshape(groups, per_group, LEAF, LEAF), near_row.reshape(groups, per_group), near_column.reshape(groups, per_group)))
    coeff_leaf = jnp.einsum("lik,lir->lkr", row_basis.astype(jnp.float32), blocked.astype(jnp.float32)).astype(jnp.bfloat16)
    coeff_middle = lift(lift_leaf, coeff_leaf)
    coeff_top = lift(lift_middle, coeff_middle)
    down_top = couple_level(coeff_top, couple_top, list_top, count_top)
    downward_middle = couple_level(coeff_middle, couple_middle, list_middle, count_middle) + descend(spread_middle, down_top)
    downward_leaf = couple_level(coeff_leaf, couple_leaf, list_leaf, count_leaf) + descend(spread_leaf, downward_middle)
    farfield_sum = jnp.einsum("qdu,qup->qdp", leaf_column_bases.astype(jnp.float32), downward_leaf, precision=lax.Precision.HIGHEST)
    return (nearfield_sum + farfield_sum).astype(jnp.bfloat16).reshape(LEAVES * LEAF, RHS)
```

```python
import jax
import jax.numpy as jnp
from jax import lax
from jax.experimental import pallas as pl
from jax.experimental.pallas import tpu as pltpu
from jax.sharding import PartitionSpec as P

F32 = jnp.float32
BF16 = jnp.bfloat16
VM = pl.BlockSpec(memory_space=pltpu.VMEM)
SM = pl.BlockSpec(memory_space=pltpu.SMEM)
HB = pl.BlockSpec(memory_space=pl.ANY)

N_PACK = 14
N_FAR_PACK = 10
CHUNKS = 8
MIDDLE_AT = 48
TOP_AT = MIDDLE_AT + 40
ZERO_AT = TOP_AT + 36


def ring(block, distance):
    count = lax.axis_size("leaf")
    return lax.ppermute(block, "leaf", [(i, (i + distance) % count) for i in range(count)])


def swapped(block):
    return lax.ppermute(block, "rhs", [(0, 1), (1, 0)])


def mm(a, b):
    return lax.dot_general(a, b, (((1,), (0,)), ((), ())), preferred_element_type=F32)


def mm_t(a, b):
    return lax.dot_general(a, b, (((1,), (1,)), ((), ())), preferred_element_type=F32)


def coeff_kernel(x, basis, lift_leaf, lift_middle, pack):
    for q in range(4):
        middles = []
        for p in (2 * q, 2 * q + 1):
            pair = [
                mm_t(x[:, l * 256 : (l + 1) * 256], basis[l]) for l in (2 * p, 2 * p + 1)
            ]
            block = jnp.concatenate(pair, axis=1).astype(BF16)
            pack[p] = block
            middles.append(mm(block, lift_leaf[p]))
        pack[8 + q] = jnp.concatenate(middles, axis=1).astype(BF16)
    for h in range(2):
        tops = [mm(pack[8 + q], lift_middle[q]) for q in (2 * h, 2 * h + 1)]
        pack[12 + h] = jnp.concatenate(tops, axis=1).astype(BF16)


def near_kernel(row, col, x, xp, blocks, own, halo, other, held, acc, sems):
    per = blocks.shape[0] // CHUNKS
    copies = [
        pltpu.make_async_copy(
            blocks.at[pl.ds(c * per, per)], held.at[pl.ds(c * per, per)], sems.at[c]
        )
        for c in range(CHUNKS)
    ]
    for c in copies:
        c.start()
    acc[...] = jnp.zeros_like(acc)
    device = row[0] // 16
    for c in range(CHUNKS):
        copies[c].wait()
        for b in range(c * per, (c + 1) * per):
            at = pl.multiple_of((row[b] - device * 16) * 256, 256)
            slot = col[b] - device * 16 + 8
            left = jnp.concatenate([x[:, pl.ds(at, 256)], xp[:, pl.ds(at, 256)]], axis=0)
            acc[slot] += mm(left, held[b])
    own[...] = acc[8:24, :64]
    halo[:8] = acc[:8, :64]
    halo[8:] = acc[24:, :64]
    other[...] = acc[:, 64:].astype(BF16)


def pack_kernel(left, own, right, up, down):
    up[0:2] = left[12:14]
    up[2:4] = own[12:14]
    up[4:10] = right[8:14]
    down[0:6] = left[8:14]
    down[6:8] = own[12:14]
    down[8:10] = right[12:14]


def halo_kernel(halo, received, low, high):
    low[...] = (halo[:8] + received[:8].astype(F32)).astype(BF16)
    high[...] = (halo[8:] + received[24:].astype(F32)).astype(BF16)


def far_kernel(
    row,
    list_leaf,
    list_middle,
    list_top,
    count_leaf,
    count_middle,
    count_top,
    pack,
    left,
    right,
    far_left,
    far_right,
    spread_middle,
    spread_leaf,
    bases,
    near,
    received,
    couple_leaf,
    couple_middle,
    couple_top,
    out,
    held_leaf,
    held_middle,
    held_top,
    dup,
    sems,
):
    copies_top = pltpu.make_async_copy(couple_top, held_top, sems.at[0])
    copies_middle = pltpu.make_async_copy(couple_middle, held_middle, sems.at[1])
    copies_leaf = [
        pltpu.make_async_copy(
            couple_leaf.at[pl.ds(4 * c, 4)], held_leaf.at[pl.ds(4 * c, 4)], sems.at[2 + c]
        )
        for c in range(4)
    ]
    copies_top.start()
    copies_middle.start()
    for c in copies_leaf:
        c.start()
    device = row[0] // 16
    first = lax.broadcasted_iota(jnp.int32, (64, 128), 1) < 64

    def double(at, block):
        turned = jnp.concatenate([block[:, 64:], block[:, :64]], axis=1)
        dup[at] = jnp.where(first, block, turned)
        dup[at + 1] = jnp.where(first, turned, block)

    for i in range(2):
        for k, (ref, at) in enumerate(
            (
                (far_left, 0),
                (far_left, 2),
                (far_left, 8),
                (left, 12),
                (pack, 12),
                (right, 12),
                (far_right, 4),
                (far_right, 6),
                (far_right, 8),
            )
        ):
            double(TOP_AT + 4 * k + 2 * i, ref[at + i])
    for i in range(4):
        for k, (ref, at) in enumerate(
            ((far_left, 4), (left, 8), (pack, 8), (right, 8), (far_right, 0))
        ):
            double(MIDDLE_AT + 8 * k + 2 * i, ref[at + i])
    for i in range(8):
        for k, ref in enumerate((left, pack, right)):
            double(16 * k + 2 * i, ref[i])
    dup[ZERO_AT] = jnp.zeros((64, 128), BF16)

    def coupled(held, lists, counts, t, base):
        live = counts[t]

        def source(j):
            return jnp.where(j < live, lists[t, j] + base, ZERO_AT)

        gathered = jnp.concatenate(
            [
                jnp.where(first, dup[source(j)], dup[source(j + 1)])
                for j in range(0, 16, 2)
            ],
            axis=1,
        )
        return mm(gathered, held[t])

    copies_top.wait()
    down_top = [
        coupled(held_top, list_top, count_top, t, TOP_AT + 16 - 4 * device).astype(BF16)
        for t in range(4)
    ]
    copies_middle.wait()
    down_middle = [
        (
            coupled(
                held_middle, list_middle, count_middle, t, MIDDLE_AT + 16 - 8 * device
            )
            + mm_t(down_top[t // 2], spread_middle[t])
        ).astype(BF16)
        for t in range(8)
    ]
    for t in range(16):
        if t % 4 == 0:
            copies_leaf[t // 4].wait()
        down = (
            coupled(held_leaf, list_leaf, count_leaf, t, 16 - 16 * device)
            + mm_t(down_middle[t // 2], spread_leaf[t])
        ).astype(BF16)
        out[t] = mm(down, bases[t]) + (near[t] + received[8 + t].astype(F32))


def final_kernel(total, from_left, from_right, out):
    for l in range(16):
        halo = from_left[l] if l < 8 else from_right[l - 8]
        out[:, l * 256 : (l + 1) * 256] = (total[l] + halo.astype(F32)).astype(BF16)


def shaped(*shape, dtype=BF16):
    return jax.ShapeDtypeStruct(shape, dtype)


def call(name, kernel, specs, outs, *args, scratch=(), mib=16, flops=0, moved=0):
    return pl.pallas_call(
        kernel,
        name=name,
        in_specs=specs,
        out_shape=outs,
        out_specs=jax.tree.map(lambda _: VM, outs),
        scratch_shapes=scratch,
        compiler_params=pltpu.CompilerParams(vmem_limit_bytes=mib << 20),
        cost_estimate=pl.CostEstimate(flops=flops, bytes_accessed=moved, transcendentals=0),
    )(*args)


def shards(
    operand,
    near_blocks,
    near_row,
    near_column,
    row_basis,
    leaf_column_bases,
    lift_leaf,
    lift_middle,
    spread_middle,
    spread_leaf,
    couple_leaf,
    couple_middle,
    couple_top,
    list_leaf,
    list_middle,
    list_top,
    count_leaf,
    count_middle,
    count_top,
):
    x = operand.T
    xp = swapped(x)
    pack = call(
        "coeff",
        coeff_kernel,
        [VM] * 4,
        shaped(N_PACK, 64, 128),
        x,
        jnp.swapaxes(row_basis, 1, 2),
        lift_leaf.reshape(8, 128, 64),
        lift_middle.reshape(4, 128, 64),
        flops=40_000_000,
        moved=2 << 20,
    )
    left, right = ring(pack, 1), ring(pack, -1)
    own, halo, other = call(
        "near",
        near_kernel,
        [SM, SM, VM, VM, HB],
        [shaped(16, 64, 256, dtype=F32), shaped(16, 64, 256, dtype=F32), shaped(32, 64, 256)],
        near_row,
        near_column,
        x,
        xp,
        near_blocks,
        scratch=[
            pltpu.VMEM((64, 256, 256), BF16),
            pltpu.VMEM((32, 128, 256), F32),
            pltpu.SemaphoreType.DMA((CHUNKS,)),
        ],
        mib=24,
        flops=1_100_000_000,
        moved=14 << 20,
    )
    received = swapped(other)
    up, down = call(
        "pack",
        pack_kernel,
        [VM] * 3,
        [shaped(N_FAR_PACK, 64, 128)] * 2,
        left,
        pack,
        right,
        moved=1 << 20,
    )
    far_left, far_right = ring(up, 3), ring(down, -3)
    low, high = call(
        "halo",
        halo_kernel,
        [VM] * 2,
        [shaped(8, 64, 256)] * 2,
        halo,
        received,
        moved=2 << 20,
    )
    from_left, from_right = ring(high, 1), ring(low, -1)
    total = call(
        "far",
        far_kernel,
        [SM] * 7 + [VM] * 10 + [HB] * 3,
        shaped(16, 64, 256, dtype=F32),
        near_row,
        list_leaf,
        list_middle,
        list_top,
        count_leaf,
        count_middle,
        count_top,
        pack,
        left,
        right,
        far_left,
        far_right,
        spread_middle,
        spread_leaf,
        jnp.swapaxes(leaf_column_bases, 1, 2),
        own,
        received,
        couple_leaf.reshape(16, 1024, 64),
        couple_middle.reshape(8, 1024, 64),
        couple_top.reshape(4, 1024, 64),
        scratch=[
            pltpu.VMEM((16, 1024, 64), BF16),
            pltpu.VMEM((8, 1024, 64), BF16),
            pltpu.VMEM((4, 1024, 64), BF16),
            pltpu.VMEM((ZERO_AT + 1, 64, 128), BF16),
            pltpu.SemaphoreType.DMA((6,)),
        ],
        mib=24,
        flops=300_000_000,
        moved=14 << 20,
    )
    out = call(
        "final",
        final_kernel,
        [VM] * 3,
        shaped(64, 4096),
        total,
        from_left,
        from_right,
        moved=2 << 20,
    )
    return out.T


def solution(mesh):
    return jax.shard_map(
        shards,
        mesh=mesh,
        in_specs=(
            P("leaf", "rhs"),
            P(("leaf", "rhs"), None, None),
            P(("leaf", "rhs")),
            P(("leaf", "rhs")),
            P("leaf", None, None),
            P("leaf", None, None),
            P("leaf", None, None),
            P("leaf", None, None),
            P("leaf", None, None),
            P("leaf", None, None),
            P("leaf", None, None, None),
            P("leaf", None, None, None),
            P("leaf", None, None, None),
            P("leaf", None),
            P("leaf", None),
            P("leaf", None),
            P("leaf"),
            P("leaf"),
            P("leaf"),
        ),
        out_specs=P("leaf", "rhs"),
        check_vma=False,
    )
```

```python
import jax
import jax.numpy as jnp
from jax import lax
from jax.experimental import pallas as pl
from jax.experimental.pallas import tpu as pltpu
from jax.sharding import PartitionSpec as P

F32 = jnp.float32
BF16 = jnp.bfloat16
VM = pl.BlockSpec(memory_space=pltpu.VMEM)
SM = pl.BlockSpec(memory_space=pltpu.SMEM)
HB = pl.BlockSpec(memory_space=pltpu.HBM)
AN = pl.BlockSpec(memory_space=pl.ANY)

N_PACK = 14
N_FAR_PACK = 10
CHUNKS = 8
FIRST = 16
TOP_AT = 40
ZERO_AT = TOP_AT + 36


def partners(count, distance, odd):
    partner = list(range(count))
    for i in range(odd, count - distance, 2):
        partner[i], partner[i + distance] = i + distance, i
    if distance == 3 and odd:
        for i, j in ((0, 2), (count - 3, count - 1)):
            partner[i], partner[j] = j, i
    return partner


def paired(block, distance, odd):
    partner = partners(lax.axis_size("leaf"), distance, odd)
    return lax.ppermute(block, "leaf", list(enumerate(partner)))


def swapped(block):
    return lax.ppermute(block, "rhs", [(0, 1), (1, 0)])


def in_hbm(array):
    return pltpu.with_memory_space_constraint(array, pltpu.HBM)


def mm(a, b):
    return lax.dot_general(a, b, (((1,), (0,)), ((), ())), preferred_element_type=F32)


def mm_t(a, b):
    return lax.dot_general(a, b, (((1,), (1,)), ((), ())), preferred_element_type=F32)


def started(*copies):
    made = [pltpu.make_async_copy(*c) for c in copies]
    for c in made:
        c.start()
    return made


def coeff_kernel(
    x_at, basis_at, lift_leaf_at, lift_middle_at, blocks, pack, x, held, basis, lift_leaf, lift_middle, sems
):
    copies = started(
        (x_at, x, sems.at[0]),
        (basis_at, basis, sems.at[1]),
        (lift_leaf_at, lift_leaf, sems.at[2]),
        (lift_middle_at, lift_middle, sems.at[3]),
        (blocks.at[pl.ds(0, FIRST)], held, sems.at[4]),
    )
    for c in copies[:4]:
        c.wait()
    for q in range(4):
        middles = []
        for p in (2 * q, 2 * q + 1):
            pair = [
                mm_t(x[:, l * 256 : (l + 1) * 256], basis[l]) for l in (2 * p, 2 * p + 1)
            ]
            block = jnp.concatenate(pair, axis=1).astype(BF16)
            pack[p] = block
            middles.append(mm(block, lift_leaf[p]))
        pack[8 + q] = jnp.concatenate(middles, axis=1).astype(BF16)
    for h in range(2):
        tops = [mm(pack[8 + q], lift_middle[q]) for q in (2 * h, 2 * h + 1)]
        pack[12 + h] = jnp.concatenate(tops, axis=1).astype(BF16)
    copies[4].wait()


def near_kernel(row_at, col_at, x, xp, held, blocks, acc, other, row, col, rest, sems):
    per = rest.shape[0] // CHUNKS
    places = started((row_at, row, sems.at[CHUNKS]), (col_at, col, sems.at[CHUNKS + 1]))
    copies = started(
        *[
            (blocks.at[pl.ds(FIRST + c * per, per)], rest.at[pl.ds(c * per, per)], sems.at[c])
            for c in range(CHUNKS)
        ]
    )
    acc[...] = jnp.zeros_like(acc)
    for c in places:
        c.wait()
    device = row[0] // 16
    for b in range(blocks.shape[0]):
        if b >= FIRST and (b - FIRST) % per == 0:
            copies[(b - FIRST) // per].wait()
        at = pl.multiple_of((row[b] - device * 16) * 256, 256)
        slot = col[b] - device * 16 + 8
        left = jnp.concatenate([x[:, pl.ds(at, 256)], xp[:, pl.ds(at, 256)]], axis=0)
        acc[slot] += mm(left, held[b] if b < FIRST else rest[b - FIRST])
    other[...] = acc[:, 64:].astype(BF16)


def pack_kernel(even, own, odd, carried, to_even, to_odd, carry):
    for out, near, far in ((to_even, even, odd), (to_odd, odd, even)):
        out[0:6] = near[8:14]
        out[6:8] = own[12:14]
        out[8:10] = far[12:14]


def place(row):
    device = row[0] // 16
    return device, 1 - 2 * (device % 2)


def first_lanes():
    return lax.broadcasted_iota(jnp.int32, (64, 128), 1) < 64


def double(dup, at, block):
    first = first_lanes()
    turned = jnp.concatenate([block[:, 64:], block[:, :64]], axis=1)
    dup[at] = jnp.where(first, block, turned)
    dup[at + 1] = jnp.where(first, turned, block)


def coupled(dup, zero_at, couple, lists, counts, t, base):
    live = counts[t]
    first = first_lanes()

    def source(j):
        return jnp.where(j < live, lists[t, j] + base, zero_at)

    gathered = jnp.concatenate(
        [jnp.where(first, dup[source(j)], dup[source(j + 1)]) for j in range(0, 16, 2)],
        axis=1,
    )
    return mm(gathered, couple[t])


def leaf_kernel(row, lists, counts, pack, even, odd, couple, far, dup):
    device, side = place(row)
    for i in range(8):
        for step, ref in ((0, pack), (side, even), (-side, odd)):
            double(dup, 16 * (1 + step) + 2 * i, ref[i])
    dup[48] = jnp.zeros((64, 128), BF16)
    for t in range(16):
        far[t] = coupled(dup, 48, couple, lists, counts, t, 16 - 16 * device)


def halo_kernel(row, acc, received, to_even, to_odd):
    device, side = place(row)
    for out, step in ((to_even, side), (to_odd, -side)):
        at = 12 + 12 * step
        out[...] = (acc[pl.ds(at, 8), :64] + received[pl.ds(at, 8)].astype(F32)).astype(BF16)


def tops_kernel(
    row,
    list_middle,
    list_top,
    count_middle,
    count_top,
    pack,
    even,
    odd,
    far_even,
    far_odd,
    couple_middle,
    couple_top,
    spread_middle,
    after,
    down_middle,
    dup,
):
    device, side = place(row)
    held = [(pack, 0, 8, 12)]
    for sign, beside, away in ((side, even, far_even), (-side, odd, far_odd)):
        held += [
            (beside, sign, 8, 12),
            (away, 2 * sign, 0, 4),
            (away, 3 * sign, None, 6),
            (away, 4 * sign, None, 8),
        ]
    for ref, step, middle_at, top_at in held:
        for i in range(2):
            double(dup, TOP_AT + 4 * (4 + step) + 2 * i, ref[top_at + i])
        if middle_at is not None:
            for i in range(4):
                double(dup, 8 * (2 + step) + 2 * i, ref[middle_at + i])
    dup[ZERO_AT] = jnp.zeros((64, 128), BF16)
    down_top = [
        coupled(
            dup, ZERO_AT, couple_top, list_top, count_top, t, TOP_AT + 16 - 4 * device
        ).astype(BF16)
        for t in range(4)
    ]
    for t in range(8):
        down_middle[t] = (
            coupled(dup, ZERO_AT, couple_middle, list_middle, count_middle, t, 16 - 8 * device)
            + mm_t(down_top[t // 2], spread_middle[t])
        ).astype(BF16)


def finish_kernel(far, down_middle, spread_leaf, bases, acc, received, out):
    for t in range(16):
        down = (far[t] + mm_t(down_middle[t // 2], spread_leaf[t])).astype(BF16)
        out[t] = mm(down, bases[t]) + (acc[8 + t, :64] + received[8 + t].astype(F32))


def final_kernel(row, total, from_even, from_odd, out):
    device, side = place(row)
    for halo, step in ((from_even, side), (from_odd, -side)):
        for k in range(8):
            l = 4 + 4 * step + k
            at = pl.multiple_of(l * 256, 256)
            out[:, pl.ds(at, 256)] = (total[l] + halo[k].astype(F32)).astype(BF16)


def shaped(*shape, dtype=BF16):
    return jax.ShapeDtypeStruct(shape, dtype)


def call(name, kernel, ins, outs, *args, scratch=(), alias=None, mib=8, work=0):
    specs = {"v": VM, "s": SM, "h": HB, "a": AN}
    kinds, made = ins.split(">")
    return pl.pallas_call(
        kernel,
        name=name,
        in_specs=[specs[k] for k in kinds],
        out_shape=outs,
        out_specs=[specs[k] for k in made],
        scratch_shapes=scratch,
        input_output_aliases=alias or {},
        compiler_params=pltpu.CompilerParams(vmem_limit_bytes=mib << 20),
        cost_estimate=pl.CostEstimate(flops=work, bytes_accessed=work // 300, transcendentals=0),
    )(*args)


def shards(
    operand,
    near_blocks,
    near_row,
    near_column,
    row_basis,
    leaf_column_bases,
    lift_leaf,
    lift_middle,
    spread_middle,
    spread_leaf,
    couple_leaf,
    couple_middle,
    couple_top,
    list_leaf,
    list_middle,
    list_top,
    count_leaf,
    count_middle,
    count_top,
):
    x = operand.T
    xp = swapped(x)
    blocks = in_hbm(near_blocks)
    pack, x_held, held = call(
        "coeff",
        coeff_kernel,
        "hhhhh>vvv",
        [shaped(N_PACK, 64, 128), shaped(64, 4096), shaped(FIRST, 256, 256)],
        in_hbm(x),
        in_hbm(jnp.swapaxes(row_basis, 1, 2)),
        in_hbm(lift_leaf.reshape(8, 128, 64)),
        in_hbm(lift_middle.reshape(4, 128, 64)),
        blocks,
        scratch=[
            pltpu.VMEM((16, 64, 256), BF16),
            pltpu.VMEM((8, 128, 64), BF16),
            pltpu.VMEM((4, 128, 64), BF16),
            pltpu.SemaphoreType.DMA((5,)),
        ],
    )
    even, odd = paired(pack, 1, 0), paired(pack, 1, 1)
    acc, other = call(
        "near",
        near_kernel,
        "hhvvvh>vv",
        [shaped(32, 128, 256, dtype=F32), shaped(32, 64, 256)],
        in_hbm(near_row),
        in_hbm(near_column),
        x_held,
        xp,
        held,
        blocks,
        scratch=[
            pltpu.SMEM((64,), jnp.int32),
            pltpu.SMEM((64,), jnp.int32),
            pltpu.VMEM((64 - FIRST, 256, 256), BF16),
            pltpu.SemaphoreType.DMA((CHUNKS + 2,)),
        ],
        mib=16,
        work=23000000000,
    )
    far_pack = shaped(N_FAR_PACK, 64, 128)
    to_even, to_odd, other = call(
        "pack",
        pack_kernel,
        "vvva>vva",
        [far_pack, far_pack, shaped(32, 64, 256)],
        even,
        pack,
        odd,
        other,
        alias={3: 2},
    )
    received = swapped(other)
    far_even, far_odd = paired(to_even, 3, 0), paired(to_odd, 3, 1)
    halos = shaped(8, 64, 256)
    [far] = call(
        "leaf",
        leaf_kernel,
        "sssvvvv>v",
        [shaped(16, 64, 64, dtype=F32)],
        near_row,
        list_leaf,
        count_leaf,
        pack,
        even,
        odd,
        couple_leaf.reshape(16, 1024, 64),
        scratch=[pltpu.VMEM((49, 64, 128), BF16)],
        work=23000000000,
    )
    halo_even, halo_odd = call(
        "halo",
        halo_kernel,
        "svv>vv",
        [halos] * 2,
        near_row,
        acc,
        received,
    )
    from_even, from_odd = paired(halo_even, 1, 0), paired(halo_odd, 1, 1)
    [down_middle] = call(
        "tops",
        tops_kernel,
        "sssssvvvvvvvva>v",
        [shaped(8, 64, 64)],
        near_row,
        list_middle,
        list_top,
        count_middle,
        count_top,
        pack,
        even,
        odd,
        far_even,
        far_odd,
        couple_middle.reshape(8, 1024, 64),
        couple_top.reshape(4, 1024, 64),
        spread_middle,
        far,
        scratch=[pltpu.VMEM((ZERO_AT + 1, 64, 128), BF16)],
        work=1150000000,
    )
    [total] = call(
        "finish",
        finish_kernel,
        "vvvvvv>v",
        [shaped(16, 64, 256, dtype=F32)],
        far,
        down_middle,
        spread_leaf,
        jnp.swapaxes(leaf_column_bases, 1, 2),
        acc,
        received,
        work=1150000000,
    )
    [out] = call(
        "final",
        final_kernel,
        "svvv>v",
        [shaped(64, 4096)],
        near_row,
        total,
        from_even,
        from_odd,
    )
    return out.T


def solution(mesh):
    return jax.shard_map(
        shards,
        mesh=mesh,
        in_specs=(
            P("leaf", "rhs"),
            P(("leaf", "rhs"), None, None),
            P(("leaf", "rhs")),
            P(("leaf", "rhs")),
            P("leaf", None, None),
            P("leaf", None, None),
            P("leaf", None, None),
            P("leaf", None, None),
            P("leaf", None, None),
            P("leaf", None, None),
            P("leaf", None, None, None),
            P("leaf", None, None, None),
            P("leaf", None, None, None),
            P("leaf", None),
            P("leaf", None),
            P("leaf", None),
            P("leaf"),
            P("leaf"),
            P("leaf"),
        ),
        out_specs=P("leaf", "rhs"),
        check_vma=False,
    )
```

```python
import jax
import jax.numpy as jnp
from jax import lax
from jax.experimental import pallas as pl
from jax.experimental.pallas import tpu as pltpu
from jax.sharding import PartitionSpec as P

F32 = jnp.float32
BF16 = jnp.bfloat16
VM = pl.BlockSpec(memory_space=pltpu.VMEM)
SM = pl.BlockSpec(memory_space=pltpu.SMEM)
HB = pl.BlockSpec(memory_space=pltpu.HBM)
AN = pl.BlockSpec(memory_space=pl.ANY)

N_PACK = 14
N_FAR_PACK = 10
CHUNKS = 8
FIRST = 16
TOP_AT = 40
ZERO_AT = TOP_AT + 36


def partners(count, distance, odd):
    partner = {(i, c): (i, 1 - c) for i in range(count) for c in (0, 1)}

    def pair(i, j, crossed):
        for c in (0, 1):
            partner[i, c], partner[j, c ^ crossed] = (j, c ^ crossed), (i, c)

    for i in range(odd, count - distance, 2):
        pair(i, i + distance, 0)
    if distance == 3 and odd:
        pair(0, 2, 1)
        pair(count - 3, count - 1, 1)
    return partner


def paired(block, distance, odd):
    partner = partners(lax.axis_size("leaf"), distance, odd)
    cores = lax.axis_size("rhs")
    route = [(i * cores + c, j * cores + d) for (i, c), (j, d) in sorted(partner.items())]
    return lax.ppermute(block, ("leaf", "rhs"), route)


def swapped(block):
    return lax.ppermute(block, "rhs", [(0, 1), (1, 0)])


def in_hbm(array):
    return pltpu.with_memory_space_constraint(array, pltpu.HBM)


def mm(a, b):
    return lax.dot_general(a, b, (((1,), (0,)), ((), ())), preferred_element_type=F32)


def mm_t(a, b):
    return lax.dot_general(a, b, (((1,), (1,)), ((), ())), preferred_element_type=F32)


def started(*copies):
    made = [pltpu.make_async_copy(*c) for c in copies]
    for c in made:
        c.start()
    return made


def coeff_kernel(
    x_at, basis_at, lift_leaf_at, lift_middle_at, blocks, pack, x, held, basis, lift_leaf, lift_middle, sems
):
    copies = started(
        (x_at, x, sems.at[0]),
        (basis_at, basis, sems.at[1]),
        (lift_leaf_at, lift_leaf, sems.at[2]),
        (lift_middle_at, lift_middle, sems.at[3]),
        (blocks.at[pl.ds(0, FIRST)], held, sems.at[4]),
    )
    for c in copies[:4]:
        c.wait()
    for q in range(4):
        middles = []
        for p in (2 * q, 2 * q + 1):
            pair = [
                mm_t(x[:, l * 256 : (l + 1) * 256], basis[l]) for l in (2 * p, 2 * p + 1)
            ]
            block = jnp.concatenate(pair, axis=1).astype(BF16)
            pack[p] = block
            middles.append(mm(block, lift_leaf[p]))
        pack[8 + q] = jnp.concatenate(middles, axis=1).astype(BF16)
    for h in range(2):
        tops = [mm(pack[8 + q], lift_middle[q]) for q in (2 * h, 2 * h + 1)]
        pack[12 + h] = jnp.concatenate(tops, axis=1).astype(BF16)
    copies[4].wait()


def near_kernel(row_at, col_at, x, xp, held, blocks, acc, other, row, col, rest, sems):
    per = rest.shape[0] // CHUNKS
    places = started((row_at, row, sems.at[CHUNKS]), (col_at, col, sems.at[CHUNKS + 1]))
    copies = started(
        *[
            (blocks.at[pl.ds(FIRST + c * per, per)], rest.at[pl.ds(c * per, per)], sems.at[c])
            for c in range(CHUNKS)
        ]
    )
    acc[...] = jnp.zeros_like(acc)
    for c in places:
        c.wait()
    device, _ = place()
    for b in range(blocks.shape[0]):
        if b >= FIRST and (b - FIRST) % per == 0:
            copies[(b - FIRST) // per].wait()
        at = pl.multiple_of((row[b] - device * 16) * 256, 256)
        slot = col[b] - device * 16 + 8
        left = jnp.concatenate([x[:, pl.ds(at, 256)], xp[:, pl.ds(at, 256)]], axis=0)
        acc[slot] += mm(left, held[b] if b < FIRST else rest[b - FIRST])
    other[...] = acc[:, 64:].astype(BF16)


def pack_kernel(even, own, odd, to_even, to_odd):
    for out, near, far in ((to_even, even, odd), (to_odd, odd, even)):
        out[0:6] = near[8:14]
        out[6:8] = own[12:14]
        out[8:10] = far[12:14]


def place():
    device = lax.axis_index("leaf")
    return device, 1 - 2 * (device % 2)


def first_lanes():
    return lax.broadcasted_iota(jnp.int32, (64, 128), 1) < 64


def double(dup, at, block):
    first = first_lanes()
    turned = jnp.concatenate([block[:, 64:], block[:, :64]], axis=1)
    dup[at] = jnp.where(first, block, turned)
    dup[at + 1] = jnp.where(first, turned, block)


def coupled(dup, zero_at, couple, lists, counts, t, base):
    live = counts[t]
    first = first_lanes()

    def source(j):
        return jnp.where(j < live, lists[t, j] + base, zero_at)

    gathered = jnp.concatenate(
        [jnp.where(first, dup[source(j)], dup[source(j + 1)]) for j in range(0, 16, 2)],
        axis=1,
    )
    return mm(gathered, couple[t])


def leaf_kernel(lists, counts, pack, even, odd, couple, far, dup):
    device, side = place()
    for i in range(8):
        for step, ref in ((0, pack), (side, even), (-side, odd)):
            double(dup, 16 * (1 + step) + 2 * i, ref[i])
    dup[48] = jnp.zeros((64, 128), BF16)
    for t in range(16):
        far[t] = coupled(dup, 48, couple, lists, counts, t, 16 - 16 * device)


def halo_kernel(acc, received, to_even, to_odd):
    device, side = place()
    for out, step in ((to_even, side), (to_odd, -side)):
        at = 12 + 12 * step
        out[...] = (acc[pl.ds(at, 8), :64] + received[pl.ds(at, 8)].astype(F32)).astype(BF16)


def tops_kernel(
    list_middle,
    list_top,
    count_middle,
    count_top,
    pack,
    even,
    odd,
    far_even,
    far_odd,
    couple_middle,
    couple_top,
    spread_middle,
    after,
    down_middle,
    dup,
):
    device, side = place()
    held = [(pack, 0, 8, 12)]
    for sign, beside, away in ((side, even, far_even), (-side, odd, far_odd)):
        held += [
            (beside, sign, 8, 12),
            (away, 2 * sign, 0, 4),
            (away, 3 * sign, None, 6),
            (away, 4 * sign, None, 8),
        ]
    for ref, step, middle_at, top_at in held:
        for i in range(2):
            double(dup, TOP_AT + 4 * (4 + step) + 2 * i, ref[top_at + i])
        if middle_at is not None:
            for i in range(4):
                double(dup, 8 * (2 + step) + 2 * i, ref[middle_at + i])
    dup[ZERO_AT] = jnp.zeros((64, 128), BF16)
    down_top = [
        coupled(
            dup, ZERO_AT, couple_top, list_top, count_top, t, TOP_AT + 16 - 4 * device
        ).astype(BF16)
        for t in range(4)
    ]
    for t in range(8):
        down_middle[t] = (
            coupled(dup, ZERO_AT, couple_middle, list_middle, count_middle, t, 16 - 8 * device)
            + mm_t(down_top[t // 2], spread_middle[t])
        ).astype(BF16)


def finish_kernel(far, down_middle, spread_leaf, bases, acc, received, out):
    for t in range(16):
        down = (far[t] + mm_t(down_middle[t // 2], spread_leaf[t])).astype(BF16)
        out[t] = mm(down, bases[t]) + (acc[8 + t, :64] + received[8 + t].astype(F32))


def final_kernel(total, from_even, from_odd, out):
    device, side = place()
    for halo, step in ((from_even, side), (from_odd, -side)):
        for k in range(8):
            l = 4 + 4 * step + k
            at = pl.multiple_of(l * 256, 256)
            out[:, pl.ds(at, 256)] = (total[l] + halo[k].astype(F32)).astype(BF16)


def shaped(*shape, dtype=BF16):
    return jax.ShapeDtypeStruct(shape, dtype)


def call(name, kernel, ins, outs, *args, scratch=(), alias=None, mib=8, work=0):
    specs = {"v": VM, "s": SM, "h": HB, "a": AN}
    kinds, made = ins.split(">")
    return pl.pallas_call(
        kernel,
        name=name,
        in_specs=[specs[k] for k in kinds],
        out_shape=outs,
        out_specs=[specs[k] for k in made],
        scratch_shapes=scratch,
        input_output_aliases=alias or {},
        compiler_params=pltpu.CompilerParams(vmem_limit_bytes=mib << 20),
        cost_estimate=pl.CostEstimate(flops=work, bytes_accessed=work // 300, transcendentals=0),
    )(*args)


def shards(
    operand,
    near_blocks,
    near_row,
    near_column,
    row_basis,
    leaf_column_bases,
    lift_leaf,
    lift_middle,
    spread_middle,
    spread_leaf,
    couple_leaf,
    couple_middle,
    couple_top,
    list_leaf,
    list_middle,
    list_top,
    count_leaf,
    count_middle,
    count_top,
):
    x = operand.T
    xp = swapped(x)
    blocks = in_hbm(near_blocks)
    pack, x_held, held = call(
        "coeff",
        coeff_kernel,
        "hhhhh>vvv",
        [shaped(N_PACK, 64, 128), shaped(64, 4096), shaped(FIRST, 256, 256)],
        in_hbm(x),
        in_hbm(jnp.swapaxes(row_basis, 1, 2)),
        in_hbm(lift_leaf.reshape(8, 128, 64)),
        in_hbm(lift_middle.reshape(4, 128, 64)),
        blocks,
        scratch=[
            pltpu.VMEM((16, 64, 256), BF16),
            pltpu.VMEM((8, 128, 64), BF16),
            pltpu.VMEM((4, 128, 64), BF16),
            pltpu.SemaphoreType.DMA((5,)),
        ],
    )
    even, odd = paired(pack, 1, 0), paired(pack, 1, 1)
    acc, other = call(
        "near",
        near_kernel,
        "hhvvvh>vv",
        [shaped(32, 128, 256, dtype=F32), shaped(32, 64, 256)],
        in_hbm(near_row),
        in_hbm(near_column),
        x_held,
        xp,
        held,
        blocks,
        scratch=[
            pltpu.SMEM((64,), jnp.int32),
            pltpu.SMEM((64,), jnp.int32),
            pltpu.VMEM((64 - FIRST, 256, 256), BF16),
            pltpu.SemaphoreType.DMA((CHUNKS + 2,)),
        ],
        mib=16,
        work=23000000000,
    )
    far_pack = shaped(N_FAR_PACK, 64, 128)
    received = swapped(other)
    to_even, to_odd = call(
        "pack",
        pack_kernel,
        "vvv>vv",
        [far_pack, far_pack],
        even,
        pack,
        odd,
        work=11500000000,
    )
    far_even, far_odd = paired(to_even, 3, 0), paired(to_odd, 3, 1)
    halos = shaped(8, 64, 256)
    [far] = call(
        "leaf",
        leaf_kernel,
        "ssvvvv>v",
        [shaped(16, 64, 64, dtype=F32)],
        list_leaf,
        count_leaf,
        pack,
        even,
        odd,
        couple_leaf.reshape(16, 1024, 64),
        scratch=[pltpu.VMEM((49, 64, 128), BF16)],
        work=23000000000,
    )
    halo_even, halo_odd = call(
        "halo",
        halo_kernel,
        "vv>vv",
        [halos] * 2,
        acc,
        received,
    )
    from_even, from_odd = paired(halo_even, 1, 0), paired(halo_odd, 1, 1)
    [down_middle] = call(
        "tops",
        tops_kernel,
        "ssssvvvvvvvva>v",
        [shaped(8, 64, 64)],
        list_middle,
        list_top,
        count_middle,
        count_top,
        pack,
        even,
        odd,
        far_even,
        far_odd,
        couple_middle.reshape(8, 1024, 64),
        couple_top.reshape(4, 1024, 64),
        spread_middle,
        far,
        scratch=[pltpu.VMEM((ZERO_AT + 1, 64, 128), BF16)],
        work=1150000000,
    )
    [total] = call(
        "finish",
        finish_kernel,
        "vvvvvv>v",
        [shaped(16, 64, 256, dtype=F32)],
        far,
        down_middle,
        spread_leaf,
        jnp.swapaxes(leaf_column_bases, 1, 2),
        acc,
        received,
        work=1150000000,
    )
    [out] = call(
        "final",
        final_kernel,
        "vvv>v",
        [shaped(64, 4096)],
        total,
        from_even,
        from_odd,
    )
    return out.T


def solution(mesh):
    return jax.shard_map(
        shards,
        mesh=mesh,
        in_specs=(
            P("leaf", "rhs"),
            P(("leaf", "rhs"), None, None),
            P(("leaf", "rhs")),
            P(("leaf", "rhs")),
            P("leaf", None, None),
            P("leaf", None, None),
            P("leaf", None, None),
            P("leaf", None, None),
            P("leaf", None, None),
            P("leaf", None, None),
            P("leaf", None, None, None),
            P("leaf", None, None, None),
            P("leaf", None, None, None),
            P("leaf", None),
            P("leaf", None),
            P("leaf", None),
            P("leaf"),
            P("leaf"),
            P("leaf"),
        ),
        out_specs=P("leaf", "rhs"),
        check_vma=False,
    )
```

```python
import jax
import jax.numpy as jnp
from jax import lax
from jax.experimental import pallas as pl
from jax.experimental.pallas import tpu as pltpu
from jax.sharding import PartitionSpec as P

F32 = jnp.float32
BF16 = jnp.bfloat16
VM = pl.BlockSpec(memory_space=pltpu.VMEM)
SM = pl.BlockSpec(memory_space=pltpu.SMEM)
HB = pl.BlockSpec(memory_space=pltpu.HBM)
AN = pl.BlockSpec(memory_space=pl.ANY)

N_PACK = 14
N_FAR_PACK = 10
CHUNKS = 8
TOP_AT = 40
ZERO_AT = TOP_AT + 36


def partners(count, distance, odd):
    partner = {(i, c): (i, 1 - c) for i in range(count) for c in (0, 1)}

    def pair(i, j, crossed):
        for c in (0, 1):
            partner[i, c], partner[j, c ^ crossed] = (j, c ^ crossed), (i, c)

    for i in range(odd, count - distance, 2):
        pair(i, i + distance, 0)
    if distance == 3 and odd:
        pair(0, 2, 1)
        pair(count - 3, count - 1, 1)
    return partner


def paired(block, distance, odd):
    partner = partners(lax.axis_size("leaf"), distance, odd)
    cores = lax.axis_size("rhs")
    route = [(i * cores + c, j * cores + d) for (i, c), (j, d) in sorted(partner.items())]
    return lax.ppermute(block, ("leaf", "rhs"), route)


def swapped(block):
    return lax.ppermute(block, "rhs", [(0, 1), (1, 0)])


def in_hbm(array):
    return pltpu.with_memory_space_constraint(array, pltpu.HBM)


def mm(a, b):
    return lax.dot_general(a, b, (((1,), (0,)), ((), ())), preferred_element_type=F32)


def mm_t(a, b):
    return lax.dot_general(a, b, (((1,), (1,)), ((), ())), preferred_element_type=F32)


def started(*copies):
    made = [pltpu.make_async_copy(*c) for c in copies]
    for c in made:
        c.start()
    return made


def mm_first(a, b):
    return lax.dot_general(a, b, (((0,), (0,)), ((), ())), preferred_element_type=F32)


def coeff_kernel(
    x_at, basis_at, lift_leaf_at, lift_middle_at, pack, x, basis, lift_leaf, lift_middle, sems
):
    parts = []
    for q in range(4):
        columns, leaves = pl.ds(q * 1024, 1024), pl.ds(q * 4, 4)
        parts.append(
            started(
                (x_at.at[:, columns], x.at[:, columns], sems.at[2 * q]),
                (basis_at.at[leaves], basis.at[leaves], sems.at[2 * q + 1]),
            )
        )
        if q == 0:
            lifts = started(
                (lift_leaf_at, lift_leaf, sems.at[8]), (lift_middle_at, lift_middle, sems.at[9])
            )
    for q in range(4):
        for c in parts[q]:
            c.wait()
        for p in (2 * q, 2 * q + 1):
            pair = [
                mm_t(x[:, l * 256 : (l + 1) * 256], basis[l]) for l in (2 * p, 2 * p + 1)
            ]
            pack[p] = jnp.concatenate(pair, axis=1).astype(BF16)
    for c in lifts:
        c.wait()
    for q in range(4):
        middles = [mm(pack[p], lift_leaf[p]) for p in (2 * q, 2 * q + 1)]
        pack[8 + q] = jnp.concatenate(middles, axis=1).astype(BF16)
    for h in range(2):
        tops = [mm(pack[8 + q], lift_middle[q]) for q in (2 * h, 2 * h + 1)]
        pack[12 + h] = jnp.concatenate(tops, axis=1).astype(BF16)


def near_kernel(row_at, col_at, x, xp, blocks, acc, other, row, col, held, sems):
    per = held.shape[0] // CHUNKS
    places = started((row_at, row, sems.at[CHUNKS]), (col_at, col, sems.at[CHUNKS + 1]))
    copies = started(
        *[
            (blocks.at[pl.ds(c * per, per)], held.at[pl.ds(c * per, per)], sems.at[c])
            for c in range(CHUNKS)
        ]
    )
    acc[...] = jnp.zeros_like(acc)
    for c in places:
        c.wait()
    device, _ = place()
    for b in range(held.shape[0]):
        if b % per == 0:
            copies[b // per].wait()
        at = pl.multiple_of((row[b] - device * 16) * 256, 256)
        slot = col[b] - device * 16 + 8
        left = jnp.concatenate([x[:, pl.ds(at, 256)], xp[:, pl.ds(at, 256)]], axis=0)
        acc[slot] += mm(left, held[b])
    other[...] = acc[:, 64:].astype(BF16)


def pack_kernel(even, own, odd, to_even, to_odd):
    for out, near, far in ((to_even, even, odd), (to_odd, odd, even)):
        out[0:6] = near[8:14]
        out[6:8] = own[12:14]
        out[8:10] = far[12:14]


def place():
    device = lax.axis_index("leaf")
    return device, 1 - 2 * (device % 2)


def first_lanes():
    return lax.broadcasted_iota(jnp.int32, (64, 128), 1) < 64


def double(dup, at, block):
    first = first_lanes()
    turned = jnp.concatenate([block[:, 64:], block[:, :64]], axis=1)
    dup[at] = jnp.where(first, block, turned)
    dup[at + 1] = jnp.where(first, turned, block)


def coupled(dup, zero_at, couple, lists, counts, t, base):
    live = counts[t]
    first = first_lanes()

    def source(j):
        return jnp.where(j < live, lists[t, j] + base, zero_at)

    gathered = jnp.concatenate(
        [jnp.where(first, dup[source(j)], dup[source(j + 1)]) for j in range(0, 16, 2)],
        axis=1,
    )
    return mm(gathered, couple[t])


def leaf_kernel(
    lists, counts, pack, even, odd, couple, spread, bases, acc, received, begun, joined, dup
):
    device, side = place()
    for i in range(8):
        for step, ref in ((0, pack), (side, even), (-side, odd)):
            double(dup, 16 * (1 + step) + 2 * i, ref[i])
    dup[48] = jnp.zeros((64, 128), BF16)
    for t in range(16):
        far = coupled(dup, 48, couple, lists, counts, t, 16 - 16 * device).astype(BF16)
        begun[t] = mm(far, bases[t]) + (acc[8 + t, :64] + received[8 + t].astype(F32))
        joined[t] = mm_first(spread[t], bases[t]).astype(BF16)


def halo_kernel(acc, received, to_even, to_odd):
    device, side = place()
    for out, step in ((to_even, side), (to_odd, -side)):
        at = 12 + 12 * step
        out[...] = (acc[pl.ds(at, 8), :64] + received[pl.ds(at, 8)].astype(F32)).astype(BF16)


def tops_kernel(
    list_middle,
    list_top,
    count_middle,
    count_top,
    pack,
    even,
    odd,
    far_even,
    far_odd,
    couple_middle,
    couple_top,
    spread_middle,
    begun,
    joined,
    total,
    dup,
):
    device, side = place()
    held = [(pack, 0, 8, 12)]
    for sign, beside, away in ((side, even, far_even), (-side, odd, far_odd)):
        held += [
            (beside, sign, 8, 12),
            (away, 2 * sign, 0, 4),
            (away, 3 * sign, None, 6),
            (away, 4 * sign, None, 8),
        ]
    for ref, step, middle_at, top_at in held:
        for i in range(2):
            double(dup, TOP_AT + 4 * (4 + step) + 2 * i, ref[top_at + i])
        if middle_at is not None:
            for i in range(4):
                double(dup, 8 * (2 + step) + 2 * i, ref[middle_at + i])
    dup[ZERO_AT] = jnp.zeros((64, 128), BF16)
    down_top = [
        coupled(
            dup, ZERO_AT, couple_top, list_top, count_top, t, TOP_AT + 16 - 4 * device
        ).astype(BF16)
        for t in range(4)
    ]
    for t in range(8):
        down_middle = (
            coupled(dup, ZERO_AT, couple_middle, list_middle, count_middle, t, 16 - 8 * device)
            + mm_t(down_top[t // 2], spread_middle[t])
        ).astype(BF16)
        for l in (2 * t, 2 * t + 1):
            total[l] = begun[l] + mm(down_middle, joined[l])


def final_kernel(total, from_even, from_odd, out):
    device, side = place()
    for halo, step in ((from_even, side), (from_odd, -side)):
        for k in range(8):
            l = 4 + 4 * step + k
            at = pl.multiple_of(l * 256, 256)
            out[:, pl.ds(at, 256)] = (total[l] + halo[k].astype(F32)).astype(BF16)


def shaped(*shape, dtype=BF16):
    return jax.ShapeDtypeStruct(shape, dtype)


def call(name, kernel, ins, outs, *args, scratch=(), alias=None, mib=8, work=0):
    specs = {"v": VM, "s": SM, "h": HB, "a": AN}
    kinds, made = ins.split(">")
    return pl.pallas_call(
        kernel,
        name=name,
        in_specs=[specs[k] for k in kinds],
        out_shape=outs,
        out_specs=[specs[k] for k in made],
        scratch_shapes=scratch,
        input_output_aliases=alias or {},
        compiler_params=pltpu.CompilerParams(vmem_limit_bytes=mib << 20),
        cost_estimate=pl.CostEstimate(flops=work, bytes_accessed=work // 300, transcendentals=0),
    )(*args)


def shards(
    operand,
    near_blocks,
    near_row,
    near_column,
    row_basis,
    leaf_column_bases,
    lift_leaf,
    lift_middle,
    spread_middle,
    spread_leaf,
    couple_leaf,
    couple_middle,
    couple_top,
    list_leaf,
    list_middle,
    list_top,
    count_leaf,
    count_middle,
    count_top,
):
    x = operand.T
    xp = swapped(x)
    pack, x_held = call(
        "coeff",
        coeff_kernel,
        "hhhh>vv",
        [shaped(N_PACK, 64, 128), shaped(64, 4096)],
        in_hbm(x),
        in_hbm(jnp.swapaxes(row_basis, 1, 2)),
        in_hbm(lift_leaf.reshape(8, 128, 64)),
        in_hbm(lift_middle.reshape(4, 128, 64)),
        scratch=[
            pltpu.VMEM((16, 64, 256), BF16),
            pltpu.VMEM((8, 128, 64), BF16),
            pltpu.VMEM((4, 128, 64), BF16),
            pltpu.SemaphoreType.DMA((10,)),
        ],
    )
    even, odd = paired(pack, 1, 0), paired(pack, 1, 1)
    acc, other = call(
        "near",
        near_kernel,
        "hhvvh>vv",
        [shaped(32, 128, 256, dtype=F32), shaped(32, 64, 256)],
        in_hbm(near_row),
        in_hbm(near_column),
        x_held,
        xp,
        in_hbm(near_blocks),
        scratch=[
            pltpu.SMEM((64,), jnp.int32),
            pltpu.SMEM((64,), jnp.int32),
            pltpu.VMEM((64, 256, 256), BF16),
            pltpu.SemaphoreType.DMA((CHUNKS + 2,)),
        ],
        mib=16,
        work=23000000000,
    )
    far_pack = shaped(N_FAR_PACK, 64, 128)
    received = swapped(other)
    to_even, to_odd = call(
        "pack",
        pack_kernel,
        "vvv>vv",
        [far_pack, far_pack],
        even,
        pack,
        odd,
        work=11500000000,
    )
    far_even, far_odd = paired(to_even, 3, 0), paired(to_odd, 3, 1)
    halos = shaped(8, 64, 256)
    sums = shaped(16, 64, 256, dtype=F32)
    begun, joined = call(
        "leaf",
        leaf_kernel,
        "ssvvvvvvvv>vv",
        [sums, shaped(16, 64, 256)],
        list_leaf,
        count_leaf,
        pack,
        even,
        odd,
        couple_leaf.reshape(16, 1024, 64),
        spread_leaf,
        jnp.swapaxes(leaf_column_bases, 1, 2),
        acc,
        received,
        scratch=[pltpu.VMEM((49, 64, 128), BF16)],
        work=23000000000,
    )
    halo_even, halo_odd = call(
        "halo",
        halo_kernel,
        "vv>vv",
        [halos] * 2,
        acc,
        received,
    )
    from_even, from_odd = paired(halo_even, 1, 0), paired(halo_odd, 1, 1)
    [total] = call(
        "tops",
        tops_kernel,
        "ssssvvvvvvvvvv>v",
        [sums],
        list_middle,
        list_top,
        count_middle,
        count_top,
        pack,
        even,
        odd,
        far_even,
        far_odd,
        couple_middle.reshape(8, 1024, 64),
        couple_top.reshape(4, 1024, 64),
        spread_middle,
        begun,
        joined,
        scratch=[pltpu.VMEM((ZERO_AT + 1, 64, 128), BF16)],
        work=2300000000,
    )
    [out] = call(
        "final",
        final_kernel,
        "vvv>v",
        [shaped(64, 4096)],
        total,
        from_even,
        from_odd,
    )
    return out.T


def solution(mesh):
    return jax.shard_map(
        shards,
        mesh=mesh,
        in_specs=(
            P("leaf", "rhs"),
            P(("leaf", "rhs"), None, None),
            P(("leaf", "rhs")),
            P(("leaf", "rhs")),
            P("leaf", None, None),
            P("leaf", None, None),
            P("leaf", None, None),
            P("leaf", None, None),
            P("leaf", None, None),
            P("leaf", None, None),
            P("leaf", None, None, None),
            P("leaf", None, None, None),
            P("leaf", None, None, None),
            P("leaf", None),
            P("leaf", None),
            P("leaf", None),
            P("leaf"),
            P("leaf"),
            P("leaf"),
        ),
        out_specs=P("leaf", "rhs"),
        check_vma=False,
    )
```
